512 devices in a mesh: row: 32 (over x_hi, z), col: 16 (over y, x_lo, core).
Axes of the slice: x: 4 (x_hi: 2, x_lo: 2; x = x_hi * 2 + x_lo), y: 4, z: 16, core: 2. Of those that a mesh axis runs over, the one named last changes fastest.
Arguments:
- traces: float32 [16, 128, 2, 1536], P('col', 'row'), may hold values from -140 to 140
- alive_mask: int32 [16, 128], P('col', 'row'), may hold values 0 or 1
- keep_mask: int32 [16, 128, 2], P('col', 'row'), may hold values 0 or 1
Outputs:
- stacked: float32 [101, 2048, 2048], P(None, 'row', 'col')
The draws below stay inside these ranges and needn't reach their ends.
All inputs are finite; a program needn't handle non-finite values. No bound on the sum of `alive_mask` or of `keep_mask` on one device may be relied on, other than what follows from the above.
Results may differ from the reference program's by a relative error of at most 0.0058.
Values may be sent and summed in bfloat16 or wider, within the bound.
No kernel may reach another device: no remote copies, remote signals or barrier semaphores. Data moves between devices by JAX's collectives and lax.ppermute only.
A program may use at most 64 MiB of HBM per device.

```python
import math
import jax
import jax.numpy as jnp
from jax import lax

WIN = 2
NT = 1536
NF = 640
SMOOTH = 65
MAXLAG = 50
LAGS = 101
NBLK = 16
CC = 128
CR = 64
CH = 2048


def draw_traces(key, part):
    key = jax.random.fold_in(key, 7)
    streams = jax.random.split(key, 6)
    shape = (NBLK, CC, WIN, NT)
    noise = jnp.clip(jax.random.normal(streams[0], shape, jnp.float32), -5.0, 5.0)
    channel_scale = jnp.exp(jax.random.uniform(streams[1], (NBLK, CC, 1, 1), jnp.float32, math.log(0.3), math.log(3.0)))
    window_scale = jnp.exp(jax.random.uniform(streams[2], (NBLK, CC, WIN, 1), jnp.float32, math.log(0.5), math.log(2.0)))
    tone_bin = jax.random.uniform(streams[3], (NBLK, CC, WIN, 1), jnp.float32, 4.0, NF - 4.0)
    tone_phase = jax.random.uniform(streams[4], (NBLK, CC, WIN, 1), jnp.float32, 0.0, 2.0 * math.pi)
    tone_size = jax.random.uniform(streams[5], (NBLK, CC, WIN, 1), jnp.float32, 0.0, 2.0)
    sample_time = jnp.arange(NT, dtype=jnp.float32)
    tone = tone_size * jnp.sin(2.0 * math.pi * tone_bin * sample_time / NT + tone_phase)
    return channel_scale * window_scale * (noise + tone)


def touch_ends(values, stream_key, low, high):
    place = [jax.random.randint(jax.random.fold_in(stream_key, axis), (), 0, length) for axis, length in enumerate(values.shape)]
    main_axis = values.shape.index(max(values.shape))
    neighbour = place[:main_axis] + [(place[main_axis] + 1) % values.shape[main_axis]] + place[main_axis + 1:]
    return values.at[tuple(place)].set(low).at[tuple(neighbour)].set(high)


def setup_inputs(seed: int = 0) -> dict:
    splits = jax.random.split(jax.random.key(seed), 4)
    return {
        "traces": draw_traces(jax.random.fold_in(splits[3], 71), 0),
        "alive_mask": touch_ends((jax.random.randint(splits[1], (NBLK, CC), 0, 16) < 15).astype(jnp.int32), jax.random.fold_in(splits[1], 1), 0, 1),
        "keep_mask": touch_ends((jax.random.randint(splits[2], (NBLK, CC, WIN), 0, 4) < 3).astype(jnp.int32), jax.random.fold_in(splits[2], 1), 0, 1),
    }


epsilon = 1e-05

def fourier_table(samples, bin_count):
    sample_index = jnp.arange(samples, dtype=jnp.int32)[:, None]
    bin_index = jnp.arange(1, bin_count + 1, dtype=jnp.int32)[None, :]
    phases = (sample_index * bin_index % samples).astype(jnp.float32) * (2.0 * math.pi / samples)
    scaling = 1.0 / math.sqrt(samples)
    return jnp.concatenate([jnp.cos(phases), -jnp.sin(phases)], axis=1) * scaling

def band_table(bin_count, span):
    column = jnp.arange(bin_count, dtype=jnp.int32)
    window_start = jnp.clip(column - span // 2, 0, bin_count - span)
    row_index = jnp.arange(bin_count, dtype=jnp.int32)[:, None]
    inside = (row_index >= window_start[None, :]) & (row_index < window_start[None, :] + span)
    return inside.astype(jnp.float32) / span

def lag_table(bin_count, samples, max_lag):
    lag_index = jnp.arange(-max_lag, max_lag + 1, dtype=jnp.int32)[:, None]
    bin_index = jnp.arange(1, bin_count + 1, dtype=jnp.int32)[None, :]
    phases = (lag_index * bin_index % samples).astype(jnp.float32) * (2.0 * math.pi / samples)
    scaling = 1.0 / math.sqrt(bin_count)
    return (jnp.concatenate([jnp.cos(phases), -jnp.sin(phases)], axis=1) * scaling).astype(jnp.bfloat16)

def whiten(series, weight, fourier, band_matrix):
    spectra = jnp.einsum('cwt,tk->wkc', series, fourier, precision=lax.Precision.HIGHEST)
    bin_count = band_matrix.shape[0]
    real_part = spectra[:, :bin_count]
    imag_part = spectra[:, bin_count:]
    amplitude = jnp.sqrt(real_part * real_part + imag_part * imag_part)
    smooth = jnp.einsum('wfc,fg->wgc', amplitude, band_matrix, precision=lax.Precision.HIGHEST)
    factor = jnp.transpose(weight)[:, None, :] / (smooth + epsilon)
    return (spectra * jnp.concatenate([factor, factor], axis=1)).astype(jnp.bfloat16)

def correlate_group(first_group, partner, lags):
    bin_count = first_group.shape[0] // 2
    first_real = first_group[:bin_count].astype(jnp.float32)[:, :, None]
    first_imag = first_group[bin_count:].astype(jnp.float32)[:, :, None]
    partner_real = partner[:bin_count].astype(jnp.float32)[:, None, :]
    partner_imag = partner[bin_count:].astype(jnp.float32)[:, None, :]
    cross = jnp.concatenate([first_real * partner_real + first_imag * partner_imag, first_imag * partner_real - first_real * partner_imag], axis=0).astype(jnp.bfloat16)
    flat = cross.reshape(2 * bin_count, first_group.shape[1] * partner.shape[1])
    result = jnp.dot(lags, flat, preferred_element_type=jnp.float32)
    return result.reshape(lags.shape[0], first_group.shape[1], partner.shape[1])

def correlate(first_block, partner, lags):
    rows = first_block.shape[1]
    group = math.gcd(rows, 16)
    groups = rows // group
    stacked_groups = jnp.transpose(first_block.reshape(first_block.shape[0], groups, group), (1, 0, 2))
    results = lax.map(lambda piece: correlate_group(piece, partner, lags), stacked_groups)
    return jnp.transpose(results, (1, 0, 2, 3)).reshape(lags.shape[0], rows, partner.shape[1])

def reference(traces, alive_mask, keep_mask):
    series = traces.reshape(CH, WIN, NT)
    weight = (alive_mask.reshape(CH)[:, None] * keep_mask.reshape(CH, WIN)).astype(jnp.float32)
    fourier = fourier_table(NT, NF)
    band_matrix = band_table(NF, SMOOTH)
    lags = lag_table(NF, NT, MAXLAG)
    spectra = whiten(series, weight, fourier, band_matrix)

    def one_block(block_index):
        offset = (block_index * CR).astype(jnp.int32)
        summed = jnp.zeros((LAGS, CR, CH), jnp.float32)
        counts = jnp.zeros((CR, CH), jnp.float32)
        for window in range(WIN):
            first_block = lax.dynamic_slice_in_dim(spectra[window], offset, CR, 1)
            summed = summed + correlate(first_block, spectra[window], lags)
            first_weight = lax.dynamic_slice_in_dim(weight[:, window], offset, CR, 0)
            counts = counts + first_weight[:, None] * weight[None, :, window]
        return summed / jnp.maximum(counts, 1.0)
    blocks = lax.map(one_block, jnp.arange(CH // CR, dtype=jnp.int32))
    return jnp.transpose(blocks, (1, 0, 2, 3)).reshape(LAGS, CH, CH)
```

```python
import math

import jax
import jax.numpy as jnp
import numpy as np
from jax import lax
from jax.experimental import pallas as pl
from jax.experimental.pallas import tpu as pltpu
from jax.sharding import PartitionSpec as P

NT = 1536
NF = 640
SMOOTH = 65
MAXLAG = 50
LAGS = 101
WIN = 2

LANE = 128
FOLD = NT // LANE
OWN = 4
SERIES = OWN * WIN
WIDTH = WIN * 2 * NF
SENT = WIDTH + LANE
QUICK = 4
SLOW = (LAGS + QUICK - 1) // QUICK
GROUP = 13
STEPS = SLOW // GROUP

epsilon = 1e-05


def split_high_low(values):
    high = values.astype(jnp.bfloat16)
    return high, (values - high.astype(jnp.float32)).astype(jnp.bfloat16)


def run_table():
    phases = 2.0 * np.pi * ((np.arange(LANE)[:, None] * np.arange(1, NF + 1)) % NT) / NT
    table = np.concatenate([np.cos(phases), np.sin(phases)], axis=1) / math.sqrt(NT)
    high = table.astype(jnp.bfloat16)
    low = (table - high.astype(np.float64)).astype(jnp.bfloat16)
    return high, low


def turn_table():
    phases = 2.0 * np.pi * ((np.arange(FOLD)[:, None] * np.arange(1, NF + 1)) % FOLD) / FOLD
    return np.concatenate([np.cos(phases), np.sin(phases)], axis=0).astype(np.float32)


def band_table():
    start = np.clip(np.arange(NF) - SMOOTH // 2, 0, NF - SMOOTH)
    row = np.arange(NF)[:, None]
    return ((row >= start) & (row < start + SMOOTH)).astype(jnp.bfloat16)


def lag_phases(lags):
    return 2.0 * np.pi * ((np.asarray(lags)[:, None] * np.arange(1, NF + 1)) % NT) / NT


def stride_table():
    phases = lag_phases(np.arange(SLOW) * QUICK - MAXLAG)
    return np.cos(phases).astype(np.float32), np.sin(phases).astype(np.float32)


def step_table():
    phases = lag_phases(-np.arange(QUICK))
    return np.cos(phases).astype(np.float32), np.sin(phases).astype(np.float32)


def whiten_kernel(alive_ref, keep_ref, traces_ref, high_ref, low_ref, turn_ref, band_ref, many_ref, one_ref):
    order = [(w, c) for w in range(WIN) for c in range(OWN)]
    series = jnp.concatenate([traces_ref[0, c, w : w + 1, :] for w, c in order], axis=0)
    runs = jnp.concatenate([series[:, LANE * r : LANE * (r + 1)] for r in range(FOLD)], axis=0)
    runs_high, runs_low = split_high_low(runs)
    high = high_ref[...]
    dot = lambda a, b: jnp.dot(a, b, preferred_element_type=jnp.float32)
    partial = dot(runs_high, high) + (dot(runs_low, high) + dot(runs_high, low_ref[...]))
    real = jnp.zeros((SERIES, NF), jnp.float32)
    imag = jnp.zeros((SERIES, NF), jnp.float32)
    for r in range(FOLD):
        cosine = partial[SERIES * r : SERIES * (r + 1), :NF]
        sine = partial[SERIES * r : SERIES * (r + 1), NF:]
        turn_cos, turn_sin = turn_ref[r : r + 1, :], turn_ref[FOLD + r : FOLD + r + 1, :]
        real = real + (cosine * turn_cos - sine * turn_sin)
        imag = imag - (cosine * turn_sin + sine * turn_cos)
    amplitude = jnp.sqrt(real * real + imag * imag)
    amp_high, rest = split_high_low(amplitude)[0], None
    rest = amplitude - amp_high.astype(jnp.float32)
    amp_mid, amp_low = split_high_low(rest)
    sums = dot(jnp.concatenate([amp_high, amp_mid, amp_low], axis=0), band_ref[...])
    total = sums[:SERIES] + (sums[SERIES : 2 * SERIES] + sums[2 * SERIES :])
    smooth = total * (1.0 / SMOOTH)
    row = lax.broadcasted_iota(jnp.int32, (SERIES, LANE), 0)
    weight = jnp.zeros((SERIES, LANE), jnp.float32)
    for s, (w, c) in enumerate(order):
        value = (alive_ref[0, c] * keep_ref[0, c * WIN + w]).astype(jnp.float32)
        weight = jnp.where(row == s, value, weight)
    factor = weight[:, :1] / (smooth + epsilon)
    lane = lax.broadcasted_iota(jnp.int32, (OWN, LANE), 1)
    tail = jnp.zeros((OWN, LANE), jnp.float32)
    pieces = []
    for w in range(WIN):
        rows = slice(OWN * w, OWN * (w + 1))
        pieces += [(real * factor)[rows], (imag * factor)[rows]]
        tail = jnp.where(lane == w, weight[rows], tail)
    sent = jnp.concatenate(pieces + [tail], axis=1).astype(jnp.bfloat16)
    one_ref[...] = sent
    for copy in range(many_ref.shape[0]):
        many_ref[copy] = sent


def whiten(traces, alive_mask, keep_mask, copies):
    high, low = run_table()
    vmem, smem = pl.BlockSpec(memory_space=pltpu.VMEM), pl.BlockSpec(memory_space=pltpu.SMEM)
    return pl.pallas_call(
        whiten_kernel,
        out_shape=(
            jax.ShapeDtypeStruct((copies, OWN, SENT), jnp.bfloat16),
            jax.ShapeDtypeStruct((OWN, SENT), jnp.bfloat16),
        ),
        in_specs=[smem, smem] + [vmem] * 5,
        out_specs=(vmem, vmem),
        compiler_params=pltpu.CompilerParams(vmem_limit_bytes=32 * 2**20),
        name="whiten",
    )(
        alive_mask,
        keep_mask.reshape(1, OWN * WIN),
        traces,
        jnp.asarray(high),
        jnp.asarray(low),
        jnp.asarray(turn_table()),
        jnp.asarray(band_table()),
    )


def rotate(values, cosine, sine, window):
    real = values[:, 2 * NF * window : 2 * NF * window + NF]
    imag = values[:, 2 * NF * window + NF : 2 * NF * (window + 1)]
    return real * cosine - imag * sine, real * sine + imag * cosine


def correlate_kernel(
    place_ref, first_ref, near_ref, far_ref, slow_cos, slow_sin, quick_cos, quick_sin,
    out_ref, first_wide, partner, turned, scale,
):
    rows, half = first_ref.shape[0], near_ref.shape[0]
    nt = (((1,), (1,)), ((), ()))

    @pl.when(pl.program_id(0) == 0)
    def _():
        lower = place_ref[0] == 0
        near, far = near_ref[...], far_ref[...]
        block = jnp.concatenate([jnp.where(lower, near, far), jnp.where(lower, far, near)], axis=0)
        first = first_ref[...]
        counts = lax.dot_general(first[:, WIDTH:], block[:, WIDTH:], nt, preferred_element_type=jnp.float32)
        scale[...] = (1.0 / math.sqrt(NF)) / jnp.maximum(counts, 1.0)
        first_wide[...] = first[:, :WIDTH].astype(jnp.float32)
        wide = block[:, :WIDTH].astype(jnp.float32)
        for q in range(QUICK):
            cosine, sine = quick_cos[q : q + 1, :], quick_sin[q : q + 1, :]
            for w in range(WIN):
                real, imag = rotate(wide, cosine, sine, w)
                at = slice(2 * half * q, 2 * half * (q + 1))
                partner[at, 2 * NF * w : 2 * NF * w + NF] = real.astype(jnp.bfloat16)
                partner[at, 2 * NF * w + NF : 2 * NF * (w + 1)] = imag.astype(jnp.bfloat16)

    for g in range(GROUP):
        stride = pl.program_id(0) * GROUP + g
        cosine, sine = slow_cos[pl.ds(stride, 1), :], slow_sin[pl.ds(stride, 1), :]
        at = slice(rows * g, rows * (g + 1))
        for w in range(WIN):
            real, imag = rotate(first_wide, cosine, sine, w)
            turned[at, 2 * NF * w : 2 * NF * w + NF] = real.astype(jnp.bfloat16)
            turned[at, 2 * NF * w + NF : 2 * NF * (w + 1)] = imag.astype(jnp.bfloat16)
    result = lax.dot_general(turned[...], partner[...], nt, preferred_element_type=jnp.float32)
    factor = scale[...]
    for g in range(GROUP):
        for q in range(QUICK):
            out_ref[QUICK * g + q] = (
                result[rows * g : rows * (g + 1), 2 * half * q : 2 * half * (q + 1)] * factor
            )


def correlate(place, first, near, far):
    rows, half = first.shape[0], near.shape[0]
    whole = lambda shape: pl.BlockSpec(shape, lambda i: (0,) * len(shape))
    return pl.pallas_call(
        correlate_kernel,
        grid=(STEPS,),
        out_shape=jax.ShapeDtypeStruct((LAGS, rows, 2 * half), jnp.float32),
        in_specs=[
            pl.BlockSpec(memory_space=pltpu.SMEM),
            whole((rows, SENT)),
            whole((half, SENT)),
            whole((half, SENT)),
            whole((SLOW, NF)),
            whole((SLOW, NF)),
            whole((QUICK, NF)),
            whole((QUICK, NF)),
        ],
        out_specs=pl.BlockSpec((GROUP * QUICK, rows, 2 * half), lambda i: (i, 0, 0)),
        scratch_shapes=[
            pltpu.VMEM((rows, WIDTH), jnp.float32),
            pltpu.VMEM((QUICK * 2 * half, WIDTH), jnp.bfloat16),
            pltpu.VMEM((GROUP * rows, WIDTH), jnp.bfloat16),
            pltpu.VMEM((rows, 2 * half), jnp.float32),
        ],
        compiler_params=pltpu.CompilerParams(vmem_limit_bytes=48 * 2**20),
        name="correlate",
    )(place, first, near, far, *map(jnp.asarray, stride_table() + step_table()))


def local(traces, alive_mask, keep_mask):
    row_count, col_count = lax.axis_size("row"), lax.axis_size("col")
    ring = row_count // 2
    many, own = whiten(traces, alive_mask, keep_mask, ring)
    per_row = row_count // 2
    moves = [
        (r * col_count + c, (2 * c + r // per_row) * col_count + r % per_row)
        for r in range(row_count)
        for c in range(col_count)
    ]
    mine = lax.ppermute(own, ("row", "col"), moves)
    lines = [list(range(ring)), list(range(ring, row_count))]
    near = lax.all_to_all(many, "row", 0, 0, axis_index_groups=lines).reshape(ring * OWN, SENT)
    far = lax.ppermute(near, "row", [(r, (r + ring) % row_count) for r in range(row_count)])
    shared = jnp.broadcast_to(mine[None], (col_count, OWN, SENT))
    first = lax.all_to_all(shared, "col", 0, 0).reshape(col_count * OWN, SENT)
    place = (lax.axis_index("row") // ring).astype(jnp.int32).reshape(1)
    return correlate(place, first, near, far)


def solution(mesh):
    placed = (P("col", "row", None, None), P("col", "row"), P("col", "row", None))
    return jax.shard_map(
        local, mesh=mesh, in_specs=placed, out_specs=P(None, "row", "col"), check_vma=False
    )
```

```python
import math

import jax
import jax.numpy as jnp
import numpy as np
from jax import lax
from jax.experimental import pallas as pl
from jax.experimental.pallas import tpu as pltpu
from jax.sharding import PartitionSpec as P

NT = 1536
NF = 640
SMOOTH = 65
MAXLAG = 50
LAGS = 101
WIN = 2

LANE = 128
FOLD = NT // LANE
OWN = 4
SERIES = OWN * WIN
WIDTH = WIN * 2 * NF
SENT = WIDTH + LANE
QUICK = 4
SLOW = (LAGS + QUICK - 1) // QUICK
GROUP = 13
STEPS = SLOW // GROUP

epsilon = 1e-05


def split_high_low(values):
    high = values.astype(jnp.bfloat16)
    return high, (values - high.astype(jnp.float32)).astype(jnp.bfloat16)


def run_table():
    phases = 2.0 * np.pi * ((np.arange(LANE)[:, None] * np.arange(1, NF + 1)) % NT) / NT
    table = np.concatenate([np.cos(phases), np.sin(phases)], axis=1) / math.sqrt(NT)
    high = table.astype(jnp.bfloat16)
    low = (table - high.astype(np.float64)).astype(jnp.bfloat16)
    return high, low


def turn_table():
    phases = 2.0 * np.pi * ((np.arange(FOLD)[:, None] * np.arange(1, NF + 1)) % FOLD) / FOLD
    return np.concatenate([np.cos(phases), np.sin(phases)], axis=0).astype(np.float32)


def band_table():
    start = np.clip(np.arange(NF) - SMOOTH // 2, 0, NF - SMOOTH)
    row = np.arange(NF)[:, None]
    return ((row >= start) & (row < start + SMOOTH)).astype(jnp.bfloat16)


def lag_phases(lags):
    return 2.0 * np.pi * ((np.asarray(lags)[:, None] * np.arange(1, NF + 1)) % NT) / NT


def stride_table():
    phases = lag_phases(np.arange(SLOW) * QUICK - MAXLAG)
    return np.cos(phases).astype(np.float32), np.sin(phases).astype(np.float32)


def step_table():
    phases = lag_phases(-np.arange(QUICK))
    return np.cos(phases).astype(np.float32), np.sin(phases).astype(np.float32)


def whiten_kernel(
    alive_hbm, keep_hbm, traces_hbm, high_hbm, low_hbm, turn_hbm, band_hbm, many_ref, one_ref,
    alive_ref, keep_ref, traces_ref, high_ref, low_ref, turn_ref, band_ref, arrived,
):
    sources = (traces_hbm, high_hbm, low_hbm, turn_hbm, alive_hbm, keep_hbm, band_hbm)
    targets = (traces_ref, high_ref, low_ref, turn_ref, alive_ref, keep_ref, band_ref)
    copies = [
        pltpu.make_async_copy(source, target, arrived.at[n])
        for n, (source, target) in enumerate(zip(sources, targets, strict=True))
    ]
    for copy in copies:
        copy.start()
    order = [(w, c) for w in range(WIN) for c in range(OWN)]
    dot = lambda a, b: jnp.dot(a, b, preferred_element_type=jnp.float32)
    for copy in copies[:4]:
        copy.wait()
    series = jnp.concatenate([traces_ref[0, c, w : w + 1, :] for w, c in order], axis=0)
    runs = jnp.concatenate([series[:, LANE * r : LANE * (r + 1)] for r in range(FOLD)], axis=0)
    runs_high, runs_low = split_high_low(runs)
    high = high_ref[...]
    partial = dot(runs_high, high) + (dot(runs_low, high) + dot(runs_high, low_ref[...]))
    real = jnp.zeros((SERIES, NF), jnp.float32)
    imag = jnp.zeros((SERIES, NF), jnp.float32)
    for r in range(FOLD):
        cosine = partial[SERIES * r : SERIES * (r + 1), :NF]
        sine = partial[SERIES * r : SERIES * (r + 1), NF:]
        turn_cos, turn_sin = turn_ref[r : r + 1, :], turn_ref[FOLD + r : FOLD + r + 1, :]
        real = real + (cosine * turn_cos - sine * turn_sin)
        imag = imag - (cosine * turn_sin + sine * turn_cos)
    amplitude = jnp.sqrt(real * real + imag * imag)
    amp_high = amplitude.astype(jnp.bfloat16)
    amp_mid, amp_low = split_high_low(amplitude - amp_high.astype(jnp.float32))
    for copy in copies[4:]:
        copy.wait()
    sums = dot(jnp.concatenate([amp_high, amp_mid, amp_low], axis=0), band_ref[...])
    total = sums[:SERIES] + (sums[SERIES : 2 * SERIES] + sums[2 * SERIES :])
    smooth = total * (1.0 / SMOOTH)
    row = lax.broadcasted_iota(jnp.int32, (SERIES, LANE), 0)
    weight = jnp.zeros((SERIES, LANE), jnp.float32)
    for s, (w, c) in enumerate(order):
        value = (alive_ref[0, c] * keep_ref[0, w, c]).astype(jnp.float32)
        weight = jnp.where(row == s, value, weight)
    factor = weight[:, :1] / (smooth + epsilon)
    lane = lax.broadcasted_iota(jnp.int32, (OWN, LANE), 1)
    tail = jnp.zeros((OWN, LANE), jnp.float32)
    pieces = []
    for w in range(WIN):
        rows = slice(OWN * w, OWN * (w + 1))
        pieces += [(real * factor)[rows], (imag * factor)[rows]]
        tail = jnp.where(lane == w, weight[rows], tail)
    sent = jnp.concatenate(pieces + [tail], axis=1).astype(jnp.bfloat16)
    one_ref[...] = sent
    for copy in range(many_ref.shape[0]):
        many_ref[copy] = sent


def whiten(traces, alive, keep, copies):
    high, low = run_table()
    shapes = [(1, OWN, WIN, NT), high.shape, low.shape, (2 * FOLD, NF), (NF, NF)]
    dtypes = [jnp.float32, jnp.bfloat16, jnp.bfloat16, jnp.float32, jnp.bfloat16]
    return pl.pallas_call(
        whiten_kernel,
        out_shape=(
            jax.ShapeDtypeStruct((copies, OWN, SENT), jnp.bfloat16),
            jax.ShapeDtypeStruct((OWN, SENT), jnp.bfloat16),
        ),
        in_specs=[pl.BlockSpec(memory_space=pltpu.HBM)] * 7,
        out_specs=(pl.BlockSpec(memory_space=pltpu.VMEM),) * 2,
        scratch_shapes=[pltpu.SMEM((1, OWN), jnp.int32), pltpu.SMEM((1, WIN, OWN), jnp.int32)]
        + [pltpu.VMEM(shape, dtype) for shape, dtype in zip(shapes, dtypes, strict=True)]
        + [pltpu.SemaphoreType.DMA((7,))],
        compiler_params=pltpu.CompilerParams(vmem_limit_bytes=60 * 2**20),
        name="whiten",
    )(
        alive,
        keep,
        traces,
        jnp.asarray(high),
        jnp.asarray(low),
        jnp.asarray(turn_table()),
        jnp.asarray(band_table()),
    )


def rotate(values, cosine, sine, window):
    real = values[:, 2 * NF * window : 2 * NF * window + NF]
    imag = values[:, 2 * NF * window + NF : 2 * NF * (window + 1)]
    return real * cosine - imag * sine, real * sine + imag * cosine


def partner_kernel(place_ref, near_ref, far_ref, quick_cos, quick_sin, turned_ref, weight_ref):
    lower = place_ref[0] == 0
    near, far = near_ref[...], far_ref[...]
    block = jnp.concatenate([jnp.where(lower, near, far), jnp.where(lower, far, near)], axis=0)
    weight_ref[...] = block[:, WIDTH:]
    wide = block[:, :WIDTH].astype(jnp.float32)
    for q in range(QUICK):
        cosine, sine = quick_cos[q : q + 1, :], quick_sin[q : q + 1, :]
        at = slice(LANE * q, LANE * (q + 1))
        for w in range(WIN):
            for part, value in enumerate(rotate(wide, cosine, sine, w)):
                start = NF * (WIN * w + part)
                turned_ref[start : start + NF, at] = jnp.transpose(value).astype(jnp.bfloat16)


def turn_partner(place, near, far):
    vmem = pl.BlockSpec(memory_space=pltpu.VMEM)
    return pl.pallas_call(
        partner_kernel,
        out_shape=(
            jax.ShapeDtypeStruct((WIDTH, QUICK * LANE), jnp.bfloat16),
            jax.ShapeDtypeStruct((LANE, LANE), jnp.bfloat16),
        ),
        in_specs=[pl.BlockSpec(memory_space=pltpu.SMEM)] + [vmem] * 4,
        out_specs=(vmem, vmem),
        compiler_params=pltpu.CompilerParams(vmem_limit_bytes=32 * 2**20),
        cost_estimate=pl.CostEstimate(flops=2 * 10**10, bytes_accessed=5 * 10**6, transcendentals=0),
        name="turn_partner",
    )(place, near, far, *map(jnp.asarray, step_table()))


def correlate_kernel(first_ref, partner_ref, weight_ref, slow_cos, slow_sin, out_ref, first_wide, turned, scale):
    rows = first_ref.shape[0]

    @pl.when(pl.program_id(0) == 0)
    def _():
        first = first_ref[...]
        counts = lax.dot_general(
            first[:, WIDTH:], weight_ref[...], (((1,), (1,)), ((), ())), preferred_element_type=jnp.float32
        )
        scale[...] = (1.0 / math.sqrt(NF)) / jnp.maximum(counts, 1.0)
        first_wide[...] = first[:, :WIDTH].astype(jnp.float32)

    for g in range(GROUP):
        stride = pl.program_id(0) * GROUP + g
        cosine, sine = slow_cos[pl.ds(stride, 1), :], slow_sin[pl.ds(stride, 1), :]
        at = slice(rows * g, rows * (g + 1))
        for w in range(WIN):
            for part, value in enumerate(rotate(first_wide, cosine, sine, w)):
                start = NF * (WIN * w + part)
                turned[at, start : start + NF] = value.astype(jnp.bfloat16)
    result = jnp.dot(turned[...], partner_ref[...], preferred_element_type=jnp.float32)
    factor = scale[...]
    for g in range(GROUP):
        for q in range(QUICK):
            out_ref[QUICK * g + q] = (
                result[rows * g : rows * (g + 1), LANE * q : LANE * (q + 1)] * factor
            )


def correlate(first, partner, weight):
    rows = first.shape[0]
    whole = lambda shape: pl.BlockSpec(shape, lambda i: (0,) * len(shape))
    return pl.pallas_call(
        correlate_kernel,
        grid=(STEPS,),
        out_shape=jax.ShapeDtypeStruct((LAGS, rows, LANE), jnp.float32),
        in_specs=[
            whole((rows, SENT)),
            whole(partner.shape),
            whole(weight.shape),
            whole((SLOW, NF)),
            whole((SLOW, NF)),
        ],
        out_specs=pl.BlockSpec((GROUP * QUICK, rows, LANE), lambda i: (i, 0, 0)),
        scratch_shapes=[
            pltpu.VMEM((rows, WIDTH), jnp.float32),
            pltpu.VMEM((GROUP * rows, WIDTH), jnp.bfloat16),
            pltpu.VMEM((rows, LANE), jnp.float32),
        ],
        compiler_params=pltpu.CompilerParams(vmem_limit_bytes=36 * 2**20),
        name="correlate",
    )(first, partner, weight, *map(jnp.asarray, stride_table()))


def local(traces, alive_mask, keep_mask):
    row_count, col_count = lax.axis_size("row"), lax.axis_size("col")
    ring = row_count // 2
    place = (lax.axis_index("row") // ring).astype(jnp.int32).reshape(1)
    many, own = whiten(traces, alive_mask, jnp.transpose(keep_mask, (0, 2, 1)), ring)
    moves = [
        (r * col_count + c, (2 * c + r // ring) * col_count + r % ring)
        for r in range(row_count)
        for c in range(col_count)
    ]
    mine = lax.ppermute(own, ("row", "col"), moves)
    lines = [list(range(ring)), list(range(ring, row_count))]
    near = lax.all_to_all(many, "row", 0, 0, axis_index_groups=lines).reshape(ring * OWN, SENT)
    far = lax.ppermute(near, "row", [(r, (r + ring) % row_count) for r in range(row_count)])
    shared = jnp.broadcast_to(mine[None], (col_count, OWN, SENT))
    first = lax.all_to_all(shared, "col", 0, 0).reshape(col_count * OWN, SENT)
    partner, weight = turn_partner(place, near, far)
    return correlate(first, partner, weight)


def solution(mesh):
    placed = (P("col", "row", None, None), P("col", "row"), P("col", "row", None))
    return jax.shard_map(
        local, mesh=mesh, in_specs=placed, out_specs=P(None, "row", "col"), check_vma=False
    )
```

```python
import math

import jax
import jax.numpy as jnp
import numpy as np
from jax import lax
from jax.experimental import pallas as pl
from jax.experimental.pallas import tpu as pltpu
from jax.sharding import PartitionSpec as P

NT = 1536
NF = 640
SMOOTH = 65
MAXLAG = 50
LAGS = 101
WIN = 2

LANE = 128
FOLD = NT // LANE
OWN = 4
SERIES = OWN * WIN
WIDTH = WIN * 2 * NF
SENT = WIDTH + LANE
QUICK = 4
SLOW = (LAGS + QUICK - 1) // QUICK
CHUNKS = (4, 8, 8, 4, 2)

epsilon = 1e-05


def split_high_low(values):
    high = values.astype(jnp.bfloat16)
    return high, (values - high.astype(jnp.float32)).astype(jnp.bfloat16)


def run_table():
    phases = 2.0 * np.pi * ((np.arange(LANE)[:, None] * np.arange(1, NF + 1)) % NT) / NT
    table = np.concatenate([np.cos(phases), np.sin(phases)], axis=1) / math.sqrt(NT)
    high = table.astype(jnp.bfloat16)
    low = (table - high.astype(np.float64)).astype(jnp.bfloat16)
    return high, low


def turn_table():
    phases = 2.0 * np.pi * ((np.arange(FOLD)[:, None] * np.arange(1, NF + 1)) % FOLD) / FOLD
    return np.concatenate([np.cos(phases), np.sin(phases)], axis=0).astype(np.float32)


def band_table():
    start = np.clip(np.arange(NF) - SMOOTH // 2, 0, NF - SMOOTH)
    row = np.arange(NF)[:, None]
    return ((row >= start) & (row < start + SMOOTH)).astype(jnp.bfloat16)


def lag_phases(lags):
    return 2.0 * np.pi * ((np.asarray(lags)[:, None] * np.arange(1, NF + 1)) % NT) / NT


def stride_table():
    phases = lag_phases(np.arange(SLOW) * QUICK - MAXLAG)
    return np.cos(phases).astype(np.float32), np.sin(phases).astype(np.float32)


def step_table():
    phases = lag_phases(-np.arange(QUICK))
    return np.cos(phases).astype(np.float32), np.sin(phases).astype(np.float32)


def whiten_kernel(
    alive_hbm, keep_hbm, traces_hbm, high_hbm, low_hbm, turn_hbm, band_hbm, many_ref, one_ref,
    alive_ref, keep_ref, traces_ref, high_ref, low_ref, turn_ref, band_ref, arrived,
):
    sources = (traces_hbm, high_hbm, low_hbm, turn_hbm, alive_hbm, keep_hbm, band_hbm)
    targets = (traces_ref, high_ref, low_ref, turn_ref, alive_ref, keep_ref, band_ref)
    copies = [
        pltpu.make_async_copy(source, target, arrived.at[n])
        for n, (source, target) in enumerate(zip(sources, targets, strict=True))
    ]
    for copy in copies:
        copy.start()
    order = [(w, c) for w in range(WIN) for c in range(OWN)]
    dot = lambda a, b: jnp.dot(a, b, preferred_element_type=jnp.float32)
    for copy in copies[:4]:
        copy.wait()
    series = jnp.concatenate([traces_ref[0, c, w : w + 1, :] for w, c in order], axis=0)
    runs = jnp.concatenate([series[:, LANE * r : LANE * (r + 1)] for r in range(FOLD)], axis=0)
    runs_high, runs_low = split_high_low(runs)
    high = high_ref[...]
    partial = dot(runs_high, high) + (dot(runs_low, high) + dot(runs_high, low_ref[...]))
    real = jnp.zeros((SERIES, NF), jnp.float32)
    imag = jnp.zeros((SERIES, NF), jnp.float32)
    for r in range(FOLD):
        cosine = partial[SERIES * r : SERIES * (r + 1), :NF]
        sine = partial[SERIES * r : SERIES * (r + 1), NF:]
        turn_cos, turn_sin = turn_ref[r : r + 1, :], turn_ref[FOLD + r : FOLD + r + 1, :]
        real = real + (cosine * turn_cos - sine * turn_sin)
        imag = imag - (cosine * turn_sin + sine * turn_cos)
    amplitude = jnp.sqrt(real * real + imag * imag)
    amp_high = amplitude.astype(jnp.bfloat16)
    amp_mid, amp_low = split_high_low(amplitude - amp_high.astype(jnp.float32))
    for copy in copies[4:]:
        copy.wait()
    sums = dot(jnp.concatenate([amp_high, amp_mid, amp_low], axis=0), band_ref[...])
    total = sums[:SERIES] + (sums[SERIES : 2 * SERIES] + sums[2 * SERIES :])
    smooth = total * (1.0 / SMOOTH)
    row = lax.broadcasted_iota(jnp.int32, (SERIES, LANE), 0)
    weight = jnp.zeros((SERIES, LANE), jnp.float32)
    for s, (w, c) in enumerate(order):
        value = (alive_ref[0, c] * keep_ref[0, w, c]).astype(jnp.float32)
        weight = jnp.where(row == s, value, weight)
    factor = weight[:, :1] / (smooth + epsilon)
    lane = lax.broadcasted_iota(jnp.int32, (OWN, LANE), 1)
    tail = jnp.zeros((OWN, LANE), jnp.float32)
    pieces = []
    for w in range(WIN):
        rows = slice(OWN * w, OWN * (w + 1))
        pieces += [(real * factor)[rows], (imag * factor)[rows]]
        tail = jnp.where(lane == w, weight[rows], tail)
    sent = jnp.concatenate(pieces + [tail], axis=1).astype(jnp.bfloat16)
    one_ref[...] = sent
    for copy in range(many_ref.shape[0]):
        many_ref[copy] = sent


def whiten(traces, alive, keep, copies):
    high, low = run_table()
    shapes = [(1, OWN, WIN, NT), high.shape, low.shape, (2 * FOLD, NF), (NF, NF)]
    dtypes = [jnp.float32, jnp.bfloat16, jnp.bfloat16, jnp.float32, jnp.bfloat16]
    return pl.pallas_call(
        whiten_kernel,
        out_shape=(
            jax.ShapeDtypeStruct((copies, OWN, SENT), jnp.bfloat16),
            jax.ShapeDtypeStruct((OWN, SENT), jnp.bfloat16),
        ),
        in_specs=[pl.BlockSpec(memory_space=pltpu.HBM)] * 7,
        out_specs=(pl.BlockSpec(memory_space=pltpu.VMEM),) * 2,
        scratch_shapes=[pltpu.SMEM((1, OWN), jnp.int32), pltpu.SMEM((1, WIN, OWN), jnp.int32)]
        + [pltpu.VMEM(shape, dtype) for shape, dtype in zip(shapes, dtypes, strict=True)]
        + [pltpu.SemaphoreType.DMA((7,))],
        compiler_params=pltpu.CompilerParams(vmem_limit_bytes=60 * 2**20),
        name="whiten",
    )(
        alive,
        keep,
        traces,
        jnp.asarray(high),
        jnp.asarray(low),
        jnp.asarray(turn_table()),
        jnp.asarray(band_table()),
    )


def repeat_kernel(one_ref, many_ref):
    sent = one_ref[...]
    for copy in range(many_ref.shape[0]):
        many_ref[copy] = sent


def repeat(one, copies):
    vmem = pl.BlockSpec(memory_space=pltpu.VMEM)
    return pl.pallas_call(
        repeat_kernel,
        out_shape=jax.ShapeDtypeStruct((copies,) + one.shape, one.dtype),
        in_specs=[vmem],
        out_specs=vmem,
        compiler_params=pltpu.CompilerParams(vmem_limit_bytes=8 * 2**20),
        cost_estimate=pl.CostEstimate(flops=2 * 10**10, bytes_accessed=10**6, transcendentals=0),
        name="repeat",
    )(one)


def rotate(values, cosine, sine, window):
    real = values[:, 2 * NF * window : 2 * NF * window + NF]
    imag = values[:, 2 * NF * window + NF : 2 * NF * (window + 1)]
    return real * cosine - imag * sine, real * sine + imag * cosine


def partner_kernel(place_ref, near_ref, far_ref, quick_cos, quick_sin, turned_ref, weight_ref):
    lower = place_ref[0] == 0
    near, far = near_ref[...], far_ref[...]
    block = jnp.concatenate([jnp.where(lower, near, far), jnp.where(lower, far, near)], axis=0)
    weight_ref[...] = block[:, WIDTH:]
    wide = block[:, :WIDTH].astype(jnp.float32)
    for q in range(QUICK):
        cosine, sine = quick_cos[q : q + 1, :], quick_sin[q : q + 1, :]
        at = slice(LANE * q, LANE * (q + 1))
        for w in range(WIN):
            for part, value in enumerate(rotate(wide, cosine, sine, w)):
                start = NF * (WIN * w + part)
                turned_ref[start : start + NF, at] = jnp.transpose(value).astype(jnp.bfloat16)


def turn_partner(place, near, far):
    vmem = pl.BlockSpec(memory_space=pltpu.VMEM)
    return pl.pallas_call(
        partner_kernel,
        out_shape=(
            jax.ShapeDtypeStruct((WIDTH, QUICK * LANE), jnp.bfloat16),
            jax.ShapeDtypeStruct((LANE, LANE), jnp.bfloat16),
        ),
        in_specs=[pl.BlockSpec(memory_space=pltpu.SMEM)] + [vmem] * 4,
        out_specs=(vmem, vmem),
        compiler_params=pltpu.CompilerParams(vmem_limit_bytes=32 * 2**20),
        cost_estimate=pl.CostEstimate(flops=2 * 10**10, bytes_accessed=5 * 10**6, transcendentals=0),
        name="turn_partner",
    )(place, near, far, *map(jnp.asarray, step_table()))


def correlate_kernel(
    first_ref, partner_ref, weight_ref, slow_cos, slow_sin, out_hbm,
    first_wide, first_tail, turned, staged, sent,
):
    rows = first_wide.shape[0]
    for s in range(rows // OWN):
        own = first_ref[s].astype(jnp.float32)
        first_wide[OWN * s : OWN * (s + 1), :] = own[:, :WIDTH]
        first_tail[OWN * s : OWN * (s + 1), :] = own[:, WIDTH:]
    counts = lax.dot_general(
        first_tail[...].astype(jnp.bfloat16), weight_ref[...], (((1,), (1,)), ((), ())),
        preferred_element_type=jnp.float32,
    )
    scale = (1.0 / math.sqrt(NF)) / jnp.maximum(counts, 1.0)

    def turn(n):
        for g in range(CHUNKS[n]):
            stride = sum(CHUNKS[:n]) + g
            cosine, sine = slow_cos[stride : stride + 1, :], slow_sin[stride : stride + 1, :]
            at = slice(rows * g, rows * (g + 1))
            for w in range(WIN):
                for part, value in enumerate(rotate(first_wide, cosine, sine, w)):
                    start = NF * (WIN * w + part)
                    turned[n % 2, at, start : start + NF] = value.astype(jnp.bfloat16)

    copies = []
    turn(0)
    for n, size in enumerate(CHUNKS):
        result = jnp.dot(
            turned[n % 2, : rows * size, :], partner_ref[...], preferred_element_type=jnp.float32
        )
        if n + 1 < len(CHUNKS):
            turn(n + 1)
        begin = sum(CHUNKS[:n]) * QUICK
        end = min(begin + size * QUICK, LAGS)
        for lag in range(begin, end):
            g, q = divmod(lag - begin, QUICK)
            staged[lag] = result[rows * g : rows * (g + 1), LANE * q : LANE * (q + 1)] * scale
        copy = pltpu.make_async_copy(
            staged.at[pl.ds(begin, end - begin)], out_hbm.at[pl.ds(begin, end - begin)], sent.at[n]
        )
        copy.start()
        copies.append(copy)
    for copy in copies:
        copy.wait()


def correlate(first, partner, weight):
    rows = first.shape[0] * first.shape[1]
    vmem = pl.BlockSpec(memory_space=pltpu.VMEM)
    return pl.pallas_call(
        correlate_kernel,
        out_shape=jax.ShapeDtypeStruct((LAGS, rows, LANE), jnp.float32),
        in_specs=[vmem] * 5,
        out_specs=pl.BlockSpec(memory_space=pltpu.HBM),
        scratch_shapes=[
            pltpu.VMEM((rows, WIDTH), jnp.float32),
            pltpu.VMEM((rows, LANE), jnp.float32),
            pltpu.VMEM((2, max(CHUNKS) * rows, WIDTH), jnp.bfloat16),
            pltpu.VMEM((LAGS, rows, LANE), jnp.float32),
            pltpu.SemaphoreType.DMA((len(CHUNKS),)),
        ],
        compiler_params=pltpu.CompilerParams(vmem_limit_bytes=36 * 2**20),
        name="correlate",
    )(first, partner, weight, *map(jnp.asarray, stride_table()))


def local(traces, alive_mask, keep_mask):
    row_count, col_count = lax.axis_size("row"), lax.axis_size("col")
    ring = row_count // 2
    place = (lax.axis_index("row") // ring).astype(jnp.int32).reshape(1)
    many, own = whiten(traces, alive_mask, jnp.transpose(keep_mask, (0, 2, 1)), ring)
    moves = [
        (r * col_count + c, (2 * c + r // ring) * col_count + r % ring)
        for r in range(row_count)
        for c in range(col_count)
    ]
    mine = lax.ppermute(own, ("row", "col"), moves)
    lines = [list(range(ring)), list(range(ring, row_count))]
    near = lax.all_to_all(many, "row", 0, 0, axis_index_groups=lines).reshape(ring * OWN, SENT)
    far = lax.ppermute(near, "row", [(r, (r + ring) % row_count) for r in range(row_count)])
    shared = repeat(mine, col_count)
    first = lax.all_to_all(shared, "col", 0, 0)
    partner, weight = turn_partner(place, near, far)
    return correlate(first, partner, weight)


def solution(mesh):
    placed = (P("col", "row", None, None), P("col", "row"), P("col", "row", None))
    return jax.shard_map(
        local, mesh=mesh, in_specs=placed, out_specs=P(None, "row", "col"), check_vma=False
    )
```

```python
import math

import jax
import jax.numpy as jnp
import numpy as np
from jax import lax
from jax.experimental import pallas as pl
from jax.experimental.pallas import tpu as pltpu
from jax.sharding import PartitionSpec as P

NT = 1536
NF = 640
SMOOTH = 65
MAXLAG = 50
LAGS = 101
WIN = 2

LANE = 128
FOLD = NT // LANE
OWN = 4
SERIES = OWN * WIN
WIDTH = WIN * 2 * NF
SENT = WIDTH + LANE
QUICK = 4
SLOW = (LAGS + QUICK - 1) // QUICK
CHUNKS = (4, 8, 8, 4, 2)

epsilon = 1e-05


def split_high_low(values):
    high = values.astype(jnp.bfloat16)
    return high, (values - high.astype(jnp.float32)).astype(jnp.bfloat16)


def run_table():
    phases = 2.0 * np.pi * ((np.arange(LANE)[:, None] * np.arange(1, NF + 1)) % NT) / NT
    table = np.concatenate([np.cos(phases), np.sin(phases)], axis=1) / math.sqrt(NT)
    high = table.astype(jnp.bfloat16)
    low = (table - high.astype(np.float64)).astype(jnp.bfloat16)
    return high, low


def turn_table():
    phases = 2.0 * np.pi * ((np.arange(FOLD)[:, None] * np.arange(1, NF + 1)) % FOLD) / FOLD
    return np.concatenate([np.cos(phases), np.sin(phases)], axis=0).astype(np.float32)


def band_table():
    start = np.clip(np.arange(NF) - SMOOTH // 2, 0, NF - SMOOTH)
    row = np.arange(NF)[:, None]
    return ((row >= start) & (row < start + SMOOTH)).astype(jnp.bfloat16)


def lag_phases(lags):
    return 2.0 * np.pi * ((np.asarray(lags)[:, None] * np.arange(1, NF + 1)) % NT) / NT


def stride_table():
    phases = lag_phases(np.arange(SLOW) * QUICK - MAXLAG)
    return np.cos(phases).astype(np.float32), np.sin(phases).astype(np.float32)


def step_table():
    phases = lag_phases(-np.arange(QUICK))
    return np.cos(phases).astype(np.float32), np.sin(phases).astype(np.float32)


def whiten_kernel(
    alive_hbm, keep_hbm, traces_hbm, high_hbm, low_hbm, turn_hbm, band_hbm, many_ref, one_ref,
    alive_ref, keep_ref, traces_ref, high_ref, low_ref, turn_ref, band_ref, arrived,
):
    sources = (traces_hbm, high_hbm, low_hbm, turn_hbm, alive_hbm, keep_hbm, band_hbm)
    targets = (traces_ref, high_ref, low_ref, turn_ref, alive_ref, keep_ref, band_ref)
    copies = [
        pltpu.make_async_copy(source, target, arrived.at[n])
        for n, (source, target) in enumerate(zip(sources, targets, strict=True))
    ]
    for copy in copies:
        copy.start()
    order = [(w, c) for w in range(WIN) for c in range(OWN)]
    dot = lambda a, b: jnp.dot(a, b, preferred_element_type=jnp.float32)
    for copy in copies[:4]:
        copy.wait()
    series = jnp.concatenate([traces_ref[0, c, w : w + 1, :] for w, c in order], axis=0)
    runs = jnp.concatenate([series[:, LANE * r : LANE * (r + 1)] for r in range(FOLD)], axis=0)
    runs_high, runs_low = split_high_low(runs)
    high = high_ref[...]
    partial = dot(runs_high, high) + (dot(runs_low, high) + dot(runs_high, low_ref[...]))
    real = jnp.zeros((SERIES, NF), jnp.float32)
    imag = jnp.zeros((SERIES, NF), jnp.float32)
    for r in range(FOLD):
        cosine = partial[SERIES * r : SERIES * (r + 1), :NF]
        sine = partial[SERIES * r : SERIES * (r + 1), NF:]
        turn_cos, turn_sin = turn_ref[r : r + 1, :], turn_ref[FOLD + r : FOLD + r + 1, :]
        real = real + (cosine * turn_cos - sine * turn_sin)
        imag = imag - (cosine * turn_sin + sine * turn_cos)
    amplitude = jnp.sqrt(real * real + imag * imag)
    amp_high = amplitude.astype(jnp.bfloat16)
    amp_mid, amp_low = split_high_low(amplitude - amp_high.astype(jnp.float32))
    for copy in copies[4:]:
        copy.wait()
    sums = dot(jnp.concatenate([amp_high, amp_mid, amp_low], axis=0), band_ref[...])
    total = sums[:SERIES] + (sums[SERIES : 2 * SERIES] + sums[2 * SERIES :])
    smooth = total * (1.0 / SMOOTH)
    row = lax.broadcasted_iota(jnp.int32, (SERIES, LANE), 0)
    weight = jnp.zeros((SERIES, LANE), jnp.float32)
    for s, (w, c) in enumerate(order):
        value = (alive_ref[0, c] * keep_ref[0, w, c]).astype(jnp.float32)
        weight = jnp.where(row == s, value, weight)
    factor = weight[:, :1] / (smooth + epsilon)
    lane = lax.broadcasted_iota(jnp.int32, (OWN, LANE), 1)
    tail = jnp.zeros((OWN, LANE), jnp.float32)
    pieces = []
    for w in range(WIN):
        rows = slice(OWN * w, OWN * (w + 1))
        pieces += [(real * factor)[rows], (imag * factor)[rows]]
        tail = jnp.where(lane == w, weight[rows], tail)
    sent = jnp.concatenate(pieces + [tail], axis=1).astype(jnp.bfloat16)
    one_ref[...] = sent
    for copy in range(many_ref.shape[0]):
        many_ref[copy] = sent


def whiten(traces, alive, keep, copies):
    high, low = run_table()
    shapes = [(1, OWN, WIN, NT), high.shape, low.shape, (2 * FOLD, NF), (NF, NF)]
    dtypes = [jnp.float32, jnp.bfloat16, jnp.bfloat16, jnp.float32, jnp.bfloat16]
    return pl.pallas_call(
        whiten_kernel,
        out_shape=(
            jax.ShapeDtypeStruct((copies, OWN, SENT), jnp.bfloat16),
            jax.ShapeDtypeStruct((OWN, SENT), jnp.bfloat16),
        ),
        in_specs=[pl.BlockSpec(memory_space=pltpu.HBM)] * 7,
        out_specs=(pl.BlockSpec(memory_space=pltpu.VMEM),) * 2,
        scratch_shapes=[pltpu.SMEM((1, OWN), jnp.int32), pltpu.SMEM((1, WIN, OWN), jnp.int32)]
        + [pltpu.VMEM(shape, dtype) for shape, dtype in zip(shapes, dtypes, strict=True)]
        + [pltpu.SemaphoreType.DMA((7,))],
        compiler_params=pltpu.CompilerParams(vmem_limit_bytes=60 * 2**20),
        name="whiten",
    )(
        alive,
        keep,
        traces,
        jnp.asarray(high),
        jnp.asarray(low),
        jnp.asarray(turn_table()),
        jnp.asarray(band_table()),
    )


def repeat_kernel(one_ref, many_ref):
    sent = one_ref[...]
    for copy in range(many_ref.shape[0]):
        many_ref[copy] = sent


def repeat(one, copies):
    vmem = pl.BlockSpec(memory_space=pltpu.VMEM)
    return pl.pallas_call(
        repeat_kernel,
        out_shape=jax.ShapeDtypeStruct((copies,) + one.shape, one.dtype),
        in_specs=[vmem],
        out_specs=vmem,
        compiler_params=pltpu.CompilerParams(vmem_limit_bytes=8 * 2**20),
        cost_estimate=pl.CostEstimate(flops=2 * 10**10, bytes_accessed=10**6, transcendentals=0),
        name="repeat",
    )(one)


def rotate(values, cosine, sine, window):
    real = values[:, 2 * NF * window : 2 * NF * window + NF]
    imag = values[:, 2 * NF * window + NF : 2 * NF * (window + 1)]
    return real * cosine - imag * sine, real * sine + imag * cosine


def partner_kernel(place_ref, near_ref, far_ref, quick_cos, quick_sin, turned_ref, weight_ref):
    lower = place_ref[0] == 0
    middle = near_ref.shape[0] // 2
    near, far = (
        jnp.concatenate([ref[middle:, :], ref[:middle, :]], axis=0) for ref in (near_ref, far_ref)
    )
    block = jnp.concatenate([jnp.where(lower, near, far), jnp.where(lower, far, near)], axis=0)
    weight_ref[...] = block[:, WIDTH:]
    wide = block[:, :WIDTH].astype(jnp.float32)
    for q in range(QUICK):
        cosine, sine = quick_cos[q : q + 1, :], quick_sin[q : q + 1, :]
        at = slice(LANE * q, LANE * (q + 1))
        for w in range(WIN):
            for part, value in enumerate(rotate(wide, cosine, sine, w)):
                start = NF * (WIN * w + part)
                turned_ref[start : start + NF, at] = jnp.transpose(value).astype(jnp.bfloat16)


def turn_partner(place, near, far):
    vmem = pl.BlockSpec(memory_space=pltpu.VMEM)
    return pl.pallas_call(
        partner_kernel,
        out_shape=(
            jax.ShapeDtypeStruct((WIDTH, QUICK * LANE), jnp.bfloat16),
            jax.ShapeDtypeStruct((LANE, LANE), jnp.bfloat16),
        ),
        in_specs=[pl.BlockSpec(memory_space=pltpu.SMEM)] + [vmem] * 4,
        out_specs=(vmem, vmem),
        compiler_params=pltpu.CompilerParams(vmem_limit_bytes=32 * 2**20),
        cost_estimate=pl.CostEstimate(flops=2 * 10**10, bytes_accessed=5 * 10**6, transcendentals=0),
        name="turn_partner",
    )(place, near, far, *map(jnp.asarray, step_table()))


def correlate_kernel(
    first_ref, partner_ref, weight_ref, slow_cos, slow_sin, out_hbm,
    first_wide, first_tail, turned, staged, sent,
):
    rows = first_wide.shape[0]
    for s in range(rows // OWN):
        own = first_ref[s].astype(jnp.float32)
        first_wide[OWN * s : OWN * (s + 1), :] = own[:, :WIDTH]
        first_tail[OWN * s : OWN * (s + 1), :] = own[:, WIDTH:]
    counts = lax.dot_general(
        first_tail[...].astype(jnp.bfloat16), weight_ref[...], (((1,), (1,)), ((), ())),
        preferred_element_type=jnp.float32,
    )
    scale = (1.0 / math.sqrt(NF)) / jnp.maximum(counts, 1.0)

    def turn(n):
        for g in range(CHUNKS[n]):
            stride = sum(CHUNKS[:n]) + g
            cosine, sine = slow_cos[stride : stride + 1, :], slow_sin[stride : stride + 1, :]
            at = slice(rows * g, rows * (g + 1))
            for w in range(WIN):
                for part, value in enumerate(rotate(first_wide, cosine, sine, w)):
                    start = NF * (WIN * w + part)
                    turned[n % 2, at, start : start + NF] = value.astype(jnp.bfloat16)

    copies = []
    turn(0)
    for n, size in enumerate(CHUNKS):
        result = jnp.dot(
            turned[n % 2, : rows * size, :], partner_ref[...], preferred_element_type=jnp.float32
        )
        if n + 1 < len(CHUNKS):
            turn(n + 1)
        begin = sum(CHUNKS[:n]) * QUICK
        end = min(begin + size * QUICK, LAGS)
        for lag in range(begin, end):
            g, q = divmod(lag - begin, QUICK)
            staged[lag] = result[rows * g : rows * (g + 1), LANE * q : LANE * (q + 1)] * scale
        copy = pltpu.make_async_copy(
            staged.at[pl.ds(begin, end - begin)], out_hbm.at[pl.ds(begin, end - begin)], sent.at[n]
        )
        copy.start()
        copies.append(copy)
    for copy in copies:
        copy.wait()


def correlate(first, partner, weight):
    rows = first.shape[0] * first.shape[1]
    vmem = pl.BlockSpec(memory_space=pltpu.VMEM)
    return pl.pallas_call(
        correlate_kernel,
        out_shape=jax.ShapeDtypeStruct((LAGS, rows, LANE), jnp.float32),
        in_specs=[vmem] * 5,
        out_specs=pl.BlockSpec(memory_space=pltpu.HBM),
        scratch_shapes=[
            pltpu.VMEM((rows, WIDTH), jnp.float32),
            pltpu.VMEM((rows, LANE), jnp.float32),
            pltpu.VMEM((2, max(CHUNKS) * rows, WIDTH), jnp.bfloat16),
            pltpu.VMEM((LAGS, rows, LANE), jnp.float32),
            pltpu.SemaphoreType.DMA((len(CHUNKS),)),
        ],
        compiler_params=pltpu.CompilerParams(vmem_limit_bytes=36 * 2**20),
        name="correlate",
    )(first, partner, weight, *map(jnp.asarray, stride_table()))


def local(traces, alive_mask, keep_mask):
    row_count, col_count = lax.axis_size("row"), lax.axis_size("col")
    ring = row_count // 2
    place = (lax.axis_index("row") // ring).astype(jnp.int32).reshape(1)
    many, own = whiten(traces, alive_mask, jnp.transpose(keep_mask, (0, 2, 1)), ring)
    moves = [
        (r * col_count + c, (2 * c + r // ring) * col_count + r % ring)
        for r in range(row_count)
        for c in range(col_count)
    ]
    mine = lax.ppermute(own, ("row", "col"), moves)
    turned = [(z + ring // 2) % ring for z in range(ring)]
    lines = [turned, [ring + z for z in turned]]
    near = lax.all_to_all(many, "row", 0, 0, axis_index_groups=lines).reshape(ring * OWN, SENT)
    far = lax.ppermute(near, "row", [(r, (r + ring) % row_count) for r in range(row_count)])
    shared = repeat(mine, col_count)
    first = lax.all_to_all(shared, "col", 0, 0)
    partner, weight = turn_partner(place, near, far)
    return correlate(first, partner, weight)


def solution(mesh):
    placed = (P("col", "row", None, None), P("col", "row"), P("col", "row", None))
    return jax.shard_map(
        local, mesh=mesh, in_specs=placed, out_specs=P(None, "row", "col"), check_vma=False
    )
```
